512 devices in a mesh: blk: 128 (over z, y, core), sub: 4 (over x).
Axes of the slice: x: 4, y: 8, z: 8, core: 2. Of those that a mesh axis runs over, the one named last changes fastest.
Arguments:
- populations: float32 [27, 512, 32, 128], P(None, 'blk', 'sub')
- destination: int32 [128, 4, 512, 1], P('blk', 'sub'), may hold values from 0 to 127; in each aligned block of 512 rows (0 to 511, 512 to 1023, ..., all dimensions but the last counted through in order) at most 8 rows name the same one
- base_cell: int32 [128, 4, 512], P('blk', 'sub'), may hold values from 0 to 2687
- offsets: float32 [128, 4, 3, 512], P('blk', 'sub'), may hold values from 0 to 1
- target: float32 [128, 4, 3, 512], P('blk', 'sub'), may hold values from -0.6 to 0.6
Outputs:
- read: float32 [27, 512, 32, 128], P(None, 'blk', 'sub')
- marker_force: float32 [128, 4, 3, 512], P('blk', 'sub')
The draws below stay inside these ranges and needn't reach their ends.
Inputs may be any that keep to these rules, and one draw needn't show every extreme that they name: `destination`: in every draw the markers of one device name each index of blk at most 8 times, and some device names some index exactly 8 times. `base_cell`: decodes as (x0 (8 - 1) + z0) * 128 + y0 with x0 < 3 and z0 < 7.
All inputs are finite; a program needn't handle non-finite values.
Results may differ from the reference program's by a relative error of at most 0.0003.
Values sent between devices are 32-bit elements; how exact they have to be, the bound alone decides.
No kernel may reach another device: no remote copies, remote signals or barrier semaphores. Data moves between devices by JAX's collectives and lax.ppermute only.
A program may use at most 64 MiB of HBM per device.

```python
import math
import jax
import jax.numpy as jnp
import numpy as np

X_DEV = 4
CELLS_Y = 128
ZC = 8
CAP = 8
NXG = 512
NZG = 32
M_DEV = 512
N_BLK = 128
N_SUB = 4


def draw_populations(key, part):
    key = jax.random.fold_in(key, 11)
    vel = np.array([[a, b, c] for a in (-1, 0, 1) for b in (-1, 0, 1) for c in (-1, 0, 1)], dtype=np.int64)
    table = np.array([8.0 / 27.0, 2.0 / 27.0, 1.0 / 54.0, 1.0 / 216.0])
    weight = jnp.asarray(table[np.abs(vel).sum(1)], jnp.float32)[:, None, None, None]
    shape = (27, NXG, NZG, CELLS_Y)
    factor = jax.random.uniform(key, shape, jnp.float32, 0.5, 1.5)
    return weight * factor


def with_ends(drawn, stream_key, smallest, largest):
    dims = drawn.shape
    spot = [jax.random.randint(jax.random.fold_in(stream_key, axis), (), 0, dims[axis]) for axis in range(len(dims))]
    drawn = drawn.at[tuple(spot)].set(smallest)
    longest = dims.index(max(dims))
    spot[longest] = (spot[longest] + 1) % dims[longest]
    return drawn.at[tuple(spot)].set(largest)


def shard_levels(rng, dims, shards, low, largest):
    loudness, own = 1.0, jax.random.fold_in(rng, 6)
    for axis_at, shards_of in shards:
        draws = jnp.exp(jax.random.uniform(jax.random.fold_in(own, axis_at), (shards_of,), jnp.float32, low / len(shards), largest / len(shards)))
        loudness = loudness * jnp.repeat(draws, dims[axis_at] // shards_of).reshape([-1 if axis == axis_at else 1 for axis in range(len(dims))])
    return loudness


def shared_out(stream_key, own, number, rows, count, top, most, slope):
    ranking = jax.random.permutation(stream_key, count)
    heavy_load, common = load_shares(count, rows * top, most, slope, True), load_shares(count, rows * top, most, slope, False)
    places = jnp.arange(count)

    def named(lengths, rotation):
        used = int((lengths > 0).sum())
        fixed = max(1, used // 4)
        passed = fixed + (places - fixed + rotation * (used - fixed)) % max(1, count - fixed)
        return jnp.zeros((count,), jnp.int32).at[ranking[jnp.where(places < fixed, places, passed)]].set(jnp.asarray(lengths, jnp.int32))

    lengths = jnp.where(number % 4 == 0, named(heavy_load, number // 4), named(common, number - number // 4 - 1))
    mixed = jax.random.permutation(jax.random.fold_in(own, 3), count)
    donor, receiver = mixed[0:count // 2 * 2:2], mixed[1:count // 2 * 2:2]
    slack = jnp.minimum(lengths[donor] - 1, most - lengths[receiver]) // 2
    slack = jnp.where((donor == ranking[0]) | (receiver == ranking[0]) | (lengths[receiver] == 0), 0, jnp.maximum(slack, 0))
    passed = jax.random.randint(jax.random.fold_in(own, 4), (count // 2,), 0, 1 << 20) % (slack + 1)
    lengths = lengths.at[donor].add(-passed).at[receiver].add(passed)
    labels = jnp.searchsorted(jnp.cumsum(lengths), jnp.arange(rows * top), side="right").astype(jnp.int32)
    grid = labels.reshape(top, rows).T
    grid = grid[jax.random.permutation(jax.random.fold_in(own, 1), rows)]
    rotation = jax.random.randint(jax.random.fold_in(own, 2), (rows, 1), 0, top)
    return jnp.take_along_axis(grid, (jnp.arange(top)[None, :] + rotation) % top, axis=1)


def load_shares(number_of, total, limit, lean, full):
    portions = [(1 << 20) // math.isqrt(rank ** lean) + 1 for rank in range(1, number_of + 1)]
    largest = limit if full else min(limit, max(-(-total // number_of), total * portions[0] // sum(portions)))
    least = 1 if total - largest >= number_of - 1 else 0
    given, surplus = [largest] + [least] * (number_of - 1), total - largest - least * (number_of - 1)
    while surplus > 0:
        movable = [i for i in range(1, number_of) if given[i] < largest] or [i for i in range(1, number_of) if given[i] < limit]
        whole, remaining = sum([portions[i] for i in movable]), surplus
        for i in movable:
            addition = min(limit - given[i], max(1, remaining * portions[i] // whole), surplus)
            given[i] = given[i] + addition
            surplus = surplus - addition
    return np.array(given)


def noise(rng, dims, scale, limit, cuts=(), held_as=jnp.bfloat16):
    values = scale * jax.random.normal(rng, dims, jnp.float32)
    if cuts:
        values = values * shard_levels(rng, dims, cuts, -0.22, 0.18)
    return jnp.clip(values, -limit, limit).astype(held_as)


def setup_inputs(seed: int = 0) -> dict:
    streams_of = jax.random.split(jax.random.key(seed), 6)
    populations = draw_populations(jax.random.fold_in(streams_of[5], 71), 0)
    destination_keys = jax.random.split(jax.random.fold_in(streams_of[1], 1), N_BLK * N_SUB * M_DEV // M_DEV)
    destination_turns = jax.random.permutation(jax.random.fold_in(streams_of[1], 3), N_BLK * N_SUB * M_DEV // M_DEV)
    destination = jax.vmap(lambda own, number: shared_out(jax.random.fold_in(streams_of[1], 2), own, number, M_DEV, N_BLK, 1, CAP, 2))(destination_keys, destination_turns).reshape((N_BLK, N_SUB, M_DEV, 1))
    base_cell = with_ends(jax.random.randint(streams_of[2], (N_BLK, N_SUB, M_DEV), 0, (X_DEV - 1) * (ZC - 1) * CELLS_Y), jax.random.fold_in(streams_of[2], 1), 0, ((X_DEV - 1) * (ZC - 1) * CELLS_Y) - 1).astype(jnp.int32)
    offsets = jnp.clip(1.0 * jax.random.uniform(streams_of[3], (N_BLK, N_SUB, 3, M_DEV), jnp.float32) ** shard_levels(streams_of[3], (N_BLK, N_SUB, 3, M_DEV), ((0, 128), (1, 4)), -0.2, 0.2), 0.0, 1.0)
    target = noise(streams_of[4], (N_BLK, N_SUB, 3, M_DEV), 0.1, 0.6, ((0, 128), (1, 4)), jnp.float32)
    return {"populations": populations, "destination": destination, "base_cell": base_cell, "offsets": offsets, "target": target}


def lattice():
    vel = np.array([[a, b, c] for a in (-1, 0, 1) for b in (-1, 0, 1) for c in (-1, 0, 1)], dtype=np.int64)
    table = np.array([8.0 / 27.0, 2.0 / 27.0, 1.0 / 54.0, 1.0 / 216.0])
    return vel, table[np.abs(vel).sum(1)]


def spread_axes(vec):
    return vec[:, None, None, None]


def collide(field, force, vel, wts):
    cx = spread_axes(jnp.asarray(vel[:, 0], jnp.float32))
    cy = spread_axes(jnp.asarray(vel[:, 1], jnp.float32))
    cz = spread_axes(jnp.asarray(vel[:, 2], jnp.float32))
    weight = spread_axes(jnp.asarray(wts, jnp.float32))
    rho = jnp.sum(field, axis=0)
    ux = (jnp.sum(field * cx, axis=0) + 0.5 * force[0]) / rho
    uy = (jnp.sum(field * cy, axis=0) + 0.5 * force[1]) / rho
    uz = (jnp.sum(field * cz, axis=0) + 0.5 * force[2]) / rho
    usq = ux * ux + uy * uy + uz * uz
    cu = cx * ux + cy * uy + cz * uz
    feq = weight * rho * (1.0 + 3.0 * cu + 4.5 * cu * cu - 1.5 * usq)
    cf = cx * force[0] + cy * force[1] + cz * force[2]
    uf = ux * force[0] + uy * force[1] + uz * force[2]
    source = weight * (3.0 * (cf - uf) + 9.0 * cu * cf)
    return field - 1.6 * (field - feq) + 0.2 * source


def fluid_velocity(field, vel):
    rho = jnp.sum(field, axis=0)
    parts = []
    for axis_pos in range(3):
        comp = spread_axes(jnp.asarray(vel[:, axis_pos], jnp.float32))
        parts.append(jnp.sum(field * comp, axis=0) / rho)
    return jnp.stack(parts)


def stencil(fracs, x_low, z_low, y_low, depth, width):
    result = []
    for dx in (0, 1):
        for dy in (0, 1):
            for dz in (0, 1):
                wx = fracs[0] if dx else 1.0 - fracs[0]
                wy = fracs[1] if dy else 1.0 - fracs[1]
                wz = fracs[2] if dz else 1.0 - fracs[2]
                flat = ((x_low + dx) * depth + z_low + dz) * width + (y_low + dy) % width
                result.append((wx * wy * wz, flat.astype(jnp.int32)))
    return result


def reference(populations, destination, base_cell, offsets, target):
    vel, wts = lattice()
    nxg, nzg, ny = populations.shape[1], populations.shape[2], populations.shape[3]
    velocity = fluid_velocity(populations, vel).reshape(3, -1)
    owner = destination[..., 0]
    sub_index = jnp.arange(N_SUB, dtype=jnp.int32)[None, :, None]
    y_low = base_cell % CELLS_Y
    rest = base_cell // CELLS_Y
    z_low = rest % (ZC - 1)
    x_low = rest // (ZC - 1)
    gx = owner * X_DEV + x_low
    gz = sub_index * ZC + z_low
    fracs = (offsets[:, :, 0], offsets[:, :, 1], offsets[:, :, 2])
    corners = stencil(fracs, gx, gz, y_low, nzg, ny)
    interp = jnp.zeros((3,) + owner.shape, jnp.float32)
    for weight, flat in corners:
        interp = interp + weight[None] * velocity[:, flat]
    force_m = 2.0 * (jnp.transpose(target, (2, 0, 1, 3)) - interp)
    field = jnp.zeros((3, nxg * nzg * ny), jnp.float32)
    for weight, flat in corners:
        field = field.at[:, flat.reshape(-1)].add((weight[None] * force_m).reshape(3, -1))
    force = field.reshape(3, nxg, nzg, ny)
    post = collide(populations, force, vel, wts)
    pieces = []
    for i in range(27):
        pieces.append(jnp.roll(post[i], (int(vel[i, 0]), int(vel[i, 2]), int(vel[i, 1])), axis=(0, 1, 2)))
    return jnp.stack(pieces), jnp.transpose(force_m, (1, 2, 0, 3))
```

```python
import jax
import jax.numpy as jnp
import numpy as np
from jax import lax
from jax.experimental import pallas as pl
from jax.experimental.pallas import tpu as pltpu
from jax.sharding import PartitionSpec as P

CAP = 8
NB = 128
NY = 128
XD = 4
ZD = 8
M = 512
F32 = jnp.float32
BF16 = jnp.bfloat16
VEL = [(a, b, c) for a in (-1, 0, 1) for b in (-1, 0, 1) for c in (-1, 0, 1)]
WTS = [(8.0 / 27.0, 2.0 / 27.0, 1.0 / 54.0, 1.0 / 216.0)[abs(a) + abs(b) + abs(c)] for a, b, c in VEL]
UP_X = [i for i in range(27) if VEL[i][0] == 1]
DOWN_X = [i for i in range(27) if VEL[i][0] == -1]
UP_Z = [i for i in range(27) if VEL[i][2] == 1]
DOWN_Z = [i for i in range(27) if VEL[i][2] == -1]
LIMIT = 12 * 1024 * 1024


def iota(shape, dim):
    return lax.broadcasted_iota(jnp.int32, shape, dim)


def split(x):
    hi = x.astype(BF16)
    return hi, (x - hi.astype(F32)).astype(BF16)


def dot_nt(a, b):
    return lax.dot_general(a, b, (((1,), (1,)), ((), ())), preferred_element_type=F32)


def dot_nn(a, b):
    return lax.dot_general(a, b, (((1,), (0,)), ((), ())), preferred_element_type=F32)


def pack_kernel(dest_ref, cell_ref, offs_ref, targ_ref, send_ref, rank_ref):
    owner = dest_ref[...]
    hot = jnp.where(iota((NB, M), 0) == owner, 1.0, 0.0)
    hot16 = hot.astype(BF16)
    before = jnp.where(iota((M, M), 0) < iota((M, M), 1), 1.0, 0.0).astype(BF16)
    count = dot_nn(hot16, before)
    rank = jnp.sum(count * hot, axis=0, keepdims=True).astype(jnp.int32)
    rank_ref[...] = rank
    chosen = jnp.where(iota((CAP, M), 0) == rank, 1.0, 0.0)
    feats = [offs_ref[k] for k in range(3)] + [targ_ref[k] for k in range(3)]
    feats += [cell_ref[...].astype(F32), jnp.ones((1, M), F32)]
    table = jnp.concatenate([chosen * f for f in feats], axis=0)
    hi, lo = split(table)
    packed = dot_nt(hot16, hi) + dot_nt(hot16, lo)
    send_ref[...] = jnp.concatenate([packed, jnp.zeros((NB, 64), F32)], axis=1)


def moments(load):
    rho = jx = jy = jz = None

    def acc(total, term, sign):
        if sign == 0:
            return total
        if total is None:
            return term if sign > 0 else -term
        return total + term if sign > 0 else total - term

    for i in range(27):
        f = load(i)
        rho = acc(rho, f, 1)
        jx = acc(jx, f, VEL[i][0])
        jy = acc(jy, f, VEL[i][1])
        jz = acc(jz, f, VEL[i][2])
    return rho, jx, jy, jz


def velocity_kernel(pop_ref, vel_ref):
    comps = [[], [], []]
    for x in range(XD):
        rho, jx, jy, jz = moments(lambda i: pop_ref[i, x])
        for c, j in enumerate((jx, jy, jz)):
            comps[c].append(j / rho)
    low = jnp.concatenate([v for comp in comps for v in comp], axis=0)
    high = pltpu.roll(low, NY - 1, 1)
    hi, lo = split(jnp.concatenate([low, high], axis=0))
    vel_ref[...] = jnp.concatenate([hi, lo], axis=0)


def signed(vec, c):
    total = None
    for v, s in zip(vec, c):
        if s:
            term = v if s > 0 else -v
            total = term if total is None else total + term
    return total


def force_kernel(recv_ref, vel_ref, pop_ref, post_ref, back_ref, up_ref, down_ref):
    table = jnp.transpose(recv_ref[...])
    feat = [table[8 * k : 8 * k + 8] for k in range(8)]
    ox, oy, oz = feat[0], feat[1], feat[2]
    valid = feat[7]
    cell = feat[6].astype(jnp.int32)
    y_low = cell & (NY - 1)
    rest = cell >> 7
    x_low = jnp.where(rest >= 7, 1, 0) + jnp.where(rest >= 14, 1, 0)
    z_low = rest - 7 * x_low
    wx = [
        jnp.where(x_low == x, 1.0 - ox, 0.0) + jnp.where(x_low == x - 1, ox, 0.0)
        for x in range(XD)
    ]
    rows = iota((NY, NB), 0)
    zrow = iota((ZD, NB), 0)
    hot = [jnp.where(rows == y_low[r : r + 1], 1.0, 0.0).astype(BF16) for r in range(CAP)]
    hot = jnp.concatenate(hot, axis=1)
    looked = dot_nn(vel_ref[...], hot)
    looked = looked[:192] + looked[192:]
    pulls = [[], [], []]
    near, far = [], []
    for r in range(CAP):
        one = slice(r, r + 1)
        zl, fz, fy = z_low[one], oz[one], oy[one]
        wz = jnp.where(zrow == zl, 1.0 - fz, 0.0) + jnp.where(zrow == zl + 1, fz, 0.0)
        wz0, wz1 = wz * (1.0 - fy), wz * fy
        w0 = [wz0 * wx[x][one] for x in range(XD)]
        w1 = [wz1 * wx[x][one] for x in range(XD)]
        lanes = slice(NB * r, NB * r + NB)
        col0, col1 = [], []
        for c in range(3):
            total = None
            for x in range(XD):
                at = 32 * c + 8 * x
                term = looked[at : at + 8, lanes] * w0[x] + looked[96 + at : 104 + at, lanes] * w1[x]
                total = term if total is None else total + term
            interp = jnp.sum(total, axis=0, keepdims=True)
            pull = 2.0 * (feat[3 + c][one] - interp) * valid[one]
            pulls[c].append(pull)
            col0 += [w0[x] * pull for x in range(XD)]
            col1 += [w1[x] * pull for x in range(XD)]
        near.append(jnp.concatenate(col0, axis=0))
        far.append(jnp.concatenate(col1, axis=0))
    reply = jnp.concatenate([p for comp in pulls for p in comp] + [jnp.zeros((NB - 24, NB), F32)], axis=0)
    back_ref[...] = jnp.transpose(reply)
    amount = jnp.concatenate([jnp.concatenate(near, axis=1), jnp.concatenate(far, axis=1)], axis=0)
    hi, lo = split(amount)
    field = dot_nt(hi, hot) + dot_nt(lo, hot)
    field = field[:96] + pltpu.roll(field[96:], 1, 1)
    for x in range(XD):
        rho, jx, jy, jz = moments(lambda i: pop_ref[i, x])
        force = [field[32 * c + 8 * x : 32 * c + 8 * x + 8] for c in range(3)]
        inv = 1.0 / rho
        u = [(j + 0.5 * f) * inv for j, f in zip((jx, jy, jz), force)]
        usq = u[0] * u[0] + u[1] * u[1] + u[2] * u[2]
        uf = u[0] * force[0] + u[1] * force[1] + u[2] * force[2]
        base = 1.6 * rho * (1.0 - 1.5 * usq) - 0.6 * uf
        ru = [rho * v for v in u]
        g = [4.8 * a + 0.6 * f for a, f in zip(ru, force)]
        h = [7.2 * a + 1.8 * f for a, f in zip(ru, force)]
        for i in range(13, 27):
            if i == 13:
                posts = ((13, WTS[13] * base),)
            else:
                c = VEL[i]
                even = base + signed(u, c) * signed(h, c)
                odd = signed(g, c)
                posts = ((i, WTS[i] * (even + odd)), (26 - i, WTS[i] * (even - odd)))
            for k, term in posts:
                out = term - 0.6 * pop_ref[k, x]
                if VEL[k][1]:
                    out = pltpu.roll(out, VEL[k][1] % NY, 1)
                post_ref[k, x] = out
                if x == XD - 1 and VEL[k][0] == 1:
                    up_ref[UP_X.index(k)] = out
                if x == 0 and VEL[k][0] == -1:
                    down_ref[DOWN_X.index(k)] = out


def shifted(post_ref, low_ref, high_ref, i, x):
    at = x - VEL[i][0]
    if at < 0:
        return low_ref[UP_X.index(i)]
    if at >= XD:
        return high_ref[DOWN_X.index(i)]
    return post_ref[i, at]


def edge_kernel(post_ref, low_ref, high_ref, up_ref, down_ref):
    up, down = [], []
    for i in UP_Z:
        for x in range(XD):
            up.append(shifted(post_ref, low_ref, high_ref, i, x)[ZD - 1 :])
    for i in DOWN_Z:
        for x in range(XD):
            down.append(shifted(post_ref, low_ref, high_ref, i, x)[:1])
    up_ref[...] = jnp.concatenate(up, axis=0)
    down_ref[...] = jnp.concatenate(down, axis=0)


def stream_kernel(post_ref, low_ref, high_ref, below_ref, above_ref, read_ref):
    row = iota((ZD, NY), 0)
    for i in range(27):
        for x in range(XD):
            v = shifted(post_ref, low_ref, high_ref, i, x)
            if VEL[i][2] == 1:
                at = 4 * UP_Z.index(i) + x
                v = jnp.where(row == 0, below_ref[at : at + 1], pltpu.roll(v, 1, 0))
            elif VEL[i][2] == -1:
                at = 4 * DOWN_Z.index(i) + x
                v = jnp.where(row == ZD - 1, above_ref[at : at + 1], pltpu.roll(v, ZD - 1, 0))
            read_ref[i, x] = v


def unpack_kernel(back_ref, dest_ref, rank_ref, out_ref):
    hot = jnp.where(iota((NB, M), 0) == dest_ref[...], 1.0, 0.0).astype(BF16)
    hi, lo = split(jnp.transpose(back_ref[...])[:24])
    found = dot_nn(hi, hot) + dot_nn(lo, hot)
    chosen = jnp.where(iota((CAP, M), 0) == rank_ref[...], 1.0, 0.0)
    for c in range(3):
        out_ref[c] = jnp.sum(found[8 * c : 8 * c + 8] * chosen, axis=0, keepdims=True)


def call(kernel, outs, *args, cost=2_000_000, name=None):
    return pl.pallas_call(
        kernel,
        out_shape=[jax.ShapeDtypeStruct(s, d) for s, d in outs],
        in_specs=[pl.BlockSpec(memory_space=pltpu.VMEM)] * len(args),
        out_specs=[pl.BlockSpec(memory_space=pltpu.VMEM)] * len(outs),
        compiler_params=pltpu.CompilerParams(vmem_limit_bytes=LIMIT),
        cost_estimate=pl.CostEstimate(flops=cost, bytes_accessed=cost, transcendentals=0),
        name=name,
    )(*args)


def exchange(x):
    out = lax.all_to_all(x.reshape(NB, 1, NY), "blk", split_axis=0, concat_axis=0, tiled=True)
    return out.reshape(NB, NY)


def ring(axis, count, step):
    return [(i, (i + step) % count) for i in range(count)]


def body(populations, destination, base_cell, offsets, target):
    dest = destination.reshape(1, M)
    cell = base_cell.reshape(1, M)
    offs = offsets.reshape(3, 1, M)
    targ = target.reshape(3, 1, M)
    send, rank = call(pack_kernel, [((NB, NY), F32), ((1, M), jnp.int32)], dest, cell, offs, targ, name="pack")
    recv = exchange(send)
    (vel,) = call(velocity_kernel, [((384, NY), BF16)], populations, name="velocity")
    face = (9, ZD, NY)
    post, back, up, down = call(
        force_kernel,
        [((27, XD, ZD, NY), F32), ((NB, NY), F32), (face, F32), (face, F32)],
        recv, vel, populations, name="force",
    )
    low = lax.ppermute(up, "blk", ring("blk", NB, 1))
    high = lax.ppermute(down, "blk", ring("blk", NB, -1))
    reply = exchange(back)
    edge = (36, NY)
    z_up, z_down = call(edge_kernel, [(edge, F32), (edge, F32)], post, low, high, name="edge")
    below = lax.ppermute(z_up, "sub", ring("sub", 4, 1))
    above = lax.ppermute(z_down, "sub", ring("sub", 4, -1))
    (read,) = call(stream_kernel, [((27, XD, ZD, NY), F32)], post, low, high, below, above, name="stream")
    (pulled,) = call(unpack_kernel, [((3, 1, M), F32)], reply, dest, rank, name="unpack")
    return read, pulled.reshape(1, 1, 3, M)


def solution(mesh):
    in_specs = (
        P(None, "blk", "sub", None),
        P("blk", "sub", None, None),
        P("blk", "sub", None),
        P("blk", "sub", None, None),
        P("blk", "sub", None, None),
    )
    out_specs = (P(None, "blk", "sub", None), P("blk", "sub", None, None))
    return jax.shard_map(body, mesh=mesh, in_specs=in_specs, out_specs=out_specs, check_vma=False)
```

```python
import jax
import jax.numpy as jnp
import numpy as np
from jax import lax
from jax.experimental import pallas as pl
from jax.experimental.pallas import tpu as pltpu
from jax.sharding import PartitionSpec as P

CAP = 8
NB = 128
NY = 128
XD = 4
ZD = 8
M = 512
F32 = jnp.float32
BF16 = jnp.bfloat16
VEL = [(a, b, c) for a in (-1, 0, 1) for b in (-1, 0, 1) for c in (-1, 0, 1)]
WTS = [(8.0 / 27.0, 2.0 / 27.0, 1.0 / 54.0, 1.0 / 216.0)[abs(a) + abs(b) + abs(c)] for a, b, c in VEL]
UP_X = [i for i in range(27) if VEL[i][0] == 1]
DOWN_X = [i for i in range(27) if VEL[i][0] == -1]
UP_Z = [i for i in range(27) if VEL[i][2] == 1]
DOWN_Z = [i for i in range(27) if VEL[i][2] == -1]
LIMIT = 12 * 1024 * 1024
FIRST = 56 * 1024 * 1024
LATE = True


def iota(shape, dim):
    return lax.broadcasted_iota(jnp.int32, shape, dim)


def split(x):
    hi = x.astype(BF16)
    return hi, (x - hi.astype(F32)).astype(BF16)


def dot_nt(a, b):
    return lax.dot_general(a, b, (((1,), (1,)), ((), ())), preferred_element_type=F32)


def dot_nn(a, b):
    return lax.dot_general(a, b, (((1,), (0,)), ((), ())), preferred_element_type=F32)


def pack_kernel(dest_ref, cell_ref, offs_ref, targ_ref, send_ref, rank_ref):
    owner = dest_ref[...]
    hot = jnp.where(iota((NB, M), 0) == owner, 1.0, 0.0)
    hot16 = hot.astype(BF16)
    before = jnp.where(iota((M, M), 0) < iota((M, M), 1), 1.0, 0.0).astype(BF16)
    count = dot_nn(hot16, before)
    rank = jnp.sum(count * hot, axis=0, keepdims=True).astype(jnp.int32)
    rank_ref[...] = rank
    chosen = jnp.where(iota((CAP, M), 0) == rank, 1.0, 0.0)
    feats = [offs_ref[k] for k in range(3)] + [targ_ref[k] for k in range(3)]
    feats += [cell_ref[...].astype(F32), jnp.ones((1, M), F32)]
    table = jnp.concatenate([chosen * f for f in feats], axis=0)
    hi, lo = split(table)
    packed = dot_nt(hot16, hi) + dot_nt(hot16, lo)
    send_ref[...] = jnp.concatenate([packed, jnp.zeros((NB, 64), F32)], axis=1)


def moments(load):
    rho = jx = jy = jz = None

    def acc(total, term, sign):
        if sign == 0:
            return total
        if total is None:
            return term if sign > 0 else -term
        return total + term if sign > 0 else total - term

    for i in range(27):
        f = load(i)
        rho = acc(rho, f, 1)
        jx = acc(jx, f, VEL[i][0])
        jy = acc(jy, f, VEL[i][1])
        jz = acc(jz, f, VEL[i][2])
    return rho, jx, jy, jz


def velocity_kernel(pop_ref, vel_ref):
    comps = [[], [], []]
    for x in range(XD):
        rho, jx, jy, jz = moments(lambda i: pop_ref[i, x])
        for c, j in enumerate((jx, jy, jz)):
            comps[c].append(j / rho)
    low = jnp.concatenate([v for comp in comps for v in comp], axis=0)
    high = pltpu.roll(low, NY - 1, 1)
    hi, lo = split(jnp.concatenate([low, high], axis=0))
    vel_ref[...] = jnp.concatenate([hi, lo], axis=0)


def signed(vec, c):
    total = None
    for v, s in zip(vec, c):
        if s:
            term = v if s > 0 else -v
            total = term if total is None else total + term
    return total


def force_kernel(recv_ref, vel_ref, pop_ref, post_ref, back_ref, pair_ref, cross_ref):
    first = (lax.axis_index("blk") & 1) == 0
    table = jnp.transpose(recv_ref[...])
    feat = [table[8 * k : 8 * k + 8] for k in range(8)]
    ox, oy, oz = feat[0], feat[1], feat[2]
    valid = feat[7]
    cell = feat[6].astype(jnp.int32)
    y_low = cell & (NY - 1)
    rest = cell >> 7
    x_low = jnp.where(rest >= 7, 1, 0) + jnp.where(rest >= 14, 1, 0)
    z_low = rest - 7 * x_low
    wx = [
        jnp.where(x_low == x, 1.0 - ox, 0.0) + jnp.where(x_low == x - 1, ox, 0.0)
        for x in range(XD)
    ]
    rows = iota((NY, NB), 0)
    zrow = iota((ZD, NB), 0)
    hot = [jnp.where(rows == y_low[r : r + 1], 1.0, 0.0).astype(BF16) for r in range(CAP)]
    hot = jnp.concatenate(hot, axis=1)
    looked = dot_nn(vel_ref[...], hot)
    looked = looked[:192] + looked[192:]
    pulls = [[], [], []]
    near, far = [], []
    for r in range(CAP):
        one = slice(r, r + 1)
        zl, fz, fy = z_low[one], oz[one], oy[one]
        wz = jnp.where(zrow == zl, 1.0 - fz, 0.0) + jnp.where(zrow == zl + 1, fz, 0.0)
        wz0, wz1 = wz * (1.0 - fy), wz * fy
        w0 = [wz0 * wx[x][one] for x in range(XD)]
        w1 = [wz1 * wx[x][one] for x in range(XD)]
        lanes = slice(NB * r, NB * r + NB)
        col0, col1 = [], []
        for c in range(3):
            total = None
            for x in range(XD):
                at = 32 * c + 8 * x
                term = looked[at : at + 8, lanes] * w0[x] + looked[96 + at : 104 + at, lanes] * w1[x]
                total = term if total is None else total + term
            interp = jnp.sum(total, axis=0, keepdims=True)
            pull = 2.0 * (feat[3 + c][one] - interp) * valid[one]
            pulls[c].append(pull)
            col0 += [w0[x] * pull for x in range(XD)]
            col1 += [w1[x] * pull for x in range(XD)]
        near.append(jnp.concatenate(col0, axis=0))
        far.append(jnp.concatenate(col1, axis=0))
    reply = jnp.concatenate([p for comp in pulls for p in comp] + [jnp.zeros((NB - 24, NB), F32)], axis=0)
    back_ref[...] = jnp.transpose(reply)
    amount = jnp.concatenate([jnp.concatenate(near, axis=1), jnp.concatenate(far, axis=1)], axis=0)
    hi, lo = split(amount)
    field = dot_nt(hi, hot) + dot_nt(lo, hot)
    field = field[:96] + pltpu.roll(field[96:], 1, 1)
    for x in range(XD):
        rho, jx, jy, jz = moments(lambda i: pop_ref[i, x])
        force = [field[32 * c + 8 * x : 32 * c + 8 * x + 8] for c in range(3)]
        inv = 1.0 / rho
        u = [(j + 0.5 * f) * inv for j, f in zip((jx, jy, jz), force)]
        usq = u[0] * u[0] + u[1] * u[1] + u[2] * u[2]
        uf = u[0] * force[0] + u[1] * force[1] + u[2] * force[2]
        base = 1.6 * rho * (1.0 - 1.5 * usq) - 0.6 * uf
        ru = [rho * v for v in u]
        g = [4.8 * a + 0.6 * f for a, f in zip(ru, force)]
        h = [7.2 * a + 1.8 * f for a, f in zip(ru, force)]
        for i in range(13, 27):
            if i == 13:
                posts = ((13, WTS[13] * base),)
            else:
                c = VEL[i]
                even = base + signed(u, c) * signed(h, c)
                odd = signed(g, c)
                posts = ((i, WTS[i] * (even + odd)), (26 - i, WTS[i] * (even - odd)))
            for k, term in posts:
                out = term - 0.6 * pop_ref[k, x]
                if VEL[k][1]:
                    out = pltpu.roll(out, VEL[k][1] % NY, 1)
                post_ref[k, x] = out


    for k in range(9):
        up, down = post_ref[UP_X[k], XD - 1], post_ref[DOWN_X[k], 0]
        pair_ref[k] = jnp.where(first, up, down)
        cross_ref[k] = jnp.where(first, down, up)


def shifted(even, post_ref, pair_ref, cross_ref, i, x):
    at = x - VEL[i][0]
    if at < 0:
        k = UP_X.index(i)
        return jnp.where(even, cross_ref[k], pair_ref[k])
    if at >= XD:
        k = DOWN_X.index(i)
        return jnp.where(even, pair_ref[k], cross_ref[k])
    return post_ref[i, at]


def edge_kernel(post_ref, low_ref, high_ref, pair_ref, cross_ref):
    even, even_z = (lax.axis_index("blk") & 1) == 0, (lax.axis_index("sub") & 1) == 0
    up, down = [], []
    for i in UP_Z:
        for x in range(XD):
            up.append(shifted(even, post_ref, low_ref, high_ref, i, x)[ZD - 1 :])
    for i in DOWN_Z:
        for x in range(XD):
            down.append(shifted(even, post_ref, low_ref, high_ref, i, x)[:1])
    up, down = jnp.concatenate(up, axis=0), jnp.concatenate(down, axis=0)
    pair_ref[...] = jnp.where(even_z, up, down)
    cross_ref[...] = jnp.where(even_z, down, up)


def stream_kernel(post_ref, low_ref, high_ref, near_ref, far_ref, read_ref):
    even, even_z = (lax.axis_index("blk") & 1) == 0, (lax.axis_index("sub") & 1) == 0
    row = iota((ZD, NY), 0)
    near, far = near_ref[...], far_ref[...]
    below, above = jnp.where(even_z, far, near), jnp.where(even_z, near, far)
    for i in range(27):
        for x in range(XD):
            v = shifted(even, post_ref, low_ref, high_ref, i, x)
            if VEL[i][2] == 1:
                at = 4 * UP_Z.index(i) + x
                v = jnp.where(row == 0, below[at : at + 1], pltpu.roll(v, 1, 0))
            elif VEL[i][2] == -1:
                at = 4 * DOWN_Z.index(i) + x
                v = jnp.where(row == ZD - 1, above[at : at + 1], pltpu.roll(v, ZD - 1, 0))
            read_ref[i, x] = v


def unpack_kernel(back_ref, dest_ref, rank_ref, out_ref):
    hot = jnp.where(iota((NB, M), 0) == dest_ref[...], 1.0, 0.0).astype(BF16)
    hi, lo = split(jnp.transpose(back_ref[...])[:24])
    found = dot_nn(hi, hot) + dot_nn(lo, hot)
    chosen = jnp.where(iota((CAP, M), 0) == rank_ref[...], 1.0, 0.0)
    for c in range(3):
        out_ref[c] = jnp.sum(found[8 * c : 8 * c + 8] * chosen, axis=0, keepdims=True)


def call(kernel, outs, *args, cost=2_000_000, name=None, limit=LIMIT):
    return pl.pallas_call(
        kernel,
        out_shape=[jax.ShapeDtypeStruct(s, d) for s, d in outs],
        in_specs=[pl.BlockSpec(memory_space=pltpu.VMEM)] * len(args),
        out_specs=[pl.BlockSpec(memory_space=pltpu.VMEM)] * len(outs),
        compiler_params=pltpu.CompilerParams(vmem_limit_bytes=limit),
        cost_estimate=pl.CostEstimate(flops=cost, bytes_accessed=cost, transcendentals=0),
        name=name,
    )(*args)


def exchange(x):
    out = lax.all_to_all(x.reshape(NB, 1, NY), "blk", split_axis=0, concat_axis=0, tiled=True)
    return out.reshape(NB, NY)


def swaps(count, first):
    ends = [(k % count, (k + 1) % count) for k in range(first, count + first, 2)]
    return ends + [(b, a) for a, b in ends]


def body(populations, destination, base_cell, offsets, target):
    dest = destination.reshape(1, M)
    cell = base_cell.reshape(1, M)
    offs = offsets.reshape(3, 1, M)
    targ = target.reshape(3, 1, M)
    send, rank = call(pack_kernel, [((NB, NY), F32), ((1, M), jnp.int32)], dest, cell, offs, targ, name="pack", limit=FIRST)
    recv = exchange(send)
    (vel,) = call(velocity_kernel, [((384, NY), BF16)], populations, name="velocity")
    face = (9, ZD, NY)
    post, back, pair, cross = call(
        force_kernel,
        [((27, XD, ZD, NY), F32), ((NB, NY), F32), (face, F32), (face, F32)],
        recv, vel, populations, name="force",
    )
    reply = exchange(back)
    pair = lax.ppermute(pair, "blk", swaps(NB, 0))
    cross = lax.ppermute(cross, "blk", swaps(NB, 1))
    edge = (36, NY)
    near, far = call(edge_kernel, [(edge, F32), (edge, F32)], post, pair, cross, name="edge")
    near = lax.ppermute(near, "sub", swaps(4, 0))
    far = lax.ppermute(far, "sub", swaps(4, 1))
    (pulled,) = call(unpack_kernel, [((3, 1, M), F32)], reply, dest, rank, name="unpack")
    if LATE:
        near, far, pulled = lax.optimization_barrier((near, far, pulled))
    (read,) = call(stream_kernel, [((27, XD, ZD, NY), F32)], post, pair, cross, near, far, name="stream")
    return read, pulled.reshape(1, 1, 3, M)


def solution(mesh):
    in_specs = (
        P(None, "blk", "sub", None),
        P("blk", "sub", None, None),
        P("blk", "sub", None),
        P("blk", "sub", None, None),
        P("blk", "sub", None, None),
    )
    out_specs = (P(None, "blk", "sub", None), P("blk", "sub", None, None))
    return jax.shard_map(body, mesh=mesh, in_specs=in_specs, out_specs=out_specs, check_vma=False)
```

```python
import jax
import jax.numpy as jnp
import numpy as np
from jax import lax
from jax.experimental import pallas as pl
from jax.experimental.pallas import tpu as pltpu
from jax.sharding import PartitionSpec as P

CAP = 8
NB = 128
NY = 128
XD = 4
ZD = 8
M = 512
F32 = jnp.float32
BF16 = jnp.bfloat16
VEL = [(a, b, c) for a in (-1, 0, 1) for b in (-1, 0, 1) for c in (-1, 0, 1)]
WTS = [(8.0 / 27.0, 2.0 / 27.0, 1.0 / 54.0, 1.0 / 216.0)[abs(a) + abs(b) + abs(c)] for a, b, c in VEL]
UP_X = [i for i in range(27) if VEL[i][0] == 1]
DOWN_X = [i for i in range(27) if VEL[i][0] == -1]
UP_Z = [i for i in range(27) if VEL[i][2] == 1]
DOWN_Z = [i for i in range(27) if VEL[i][2] == -1]
LIMIT = 12 * 1024 * 1024
FIRST = 56 * 1024 * 1024
TURN = 112
EDGE = 2_000_000_000


def iota(shape, dim):
    return lax.broadcasted_iota(jnp.int32, shape, dim)


def split(x):
    hi = x.astype(BF16)
    return hi, (x - hi.astype(F32)).astype(BF16)


def dot_nt(a, b):
    return lax.dot_general(a, b, (((1,), (1,)), ((), ())), preferred_element_type=F32)


def dot_nn(a, b):
    return lax.dot_general(a, b, (((1,), (0,)), ((), ())), preferred_element_type=F32)


def pack_kernel(dest_ref, cell_ref, offs_ref, targ_ref, send_ref, row_ref, rank_ref):
    owner = (dest_ref[...] - TURN) & (NB - 1)
    row_ref[...] = owner
    hot = jnp.where(iota((NB, M), 0) == owner, 1.0, 0.0)
    hot16 = hot.astype(BF16)
    blocks = [slice(NB * k, NB * k + NB) for k in range(M // NB)]
    column = iota((NB, 2 * NB), 1)
    before = jnp.where((iota((NB, 2 * NB), 0) < column) | (column >= NB), 1.0, 0.0).astype(BF16)
    count = dot_nn(jnp.concatenate([hot16[:, k] for k in blocks], axis=0), before)
    ranks, passed = [], 0.0
    for k in blocks:
        ranks.append(jnp.sum((count[k, :NB] + passed) * hot[:, k], axis=0, keepdims=True))
        passed = passed + count[k, NB:]
    rank = jnp.concatenate(ranks, axis=1).astype(jnp.int32)
    rank_ref[...] = rank
    chosen = jnp.where(iota((CAP, M), 0) == rank, 1.0, 0.0)
    feats = [offs_ref[k] for k in range(3)] + [targ_ref[k] for k in range(3)]
    feats += [cell_ref[...].astype(F32), jnp.ones((1, M), F32)]
    table = jnp.concatenate([chosen * f for f in feats], axis=0)
    hi, lo = split(table)
    packed = dot_nt(hot16, jnp.concatenate([hi, lo], axis=0))
    send_ref[...] = packed + pltpu.roll(packed, 64, 1)


def moments(load):
    rho = jx = jy = jz = None

    def acc(total, term, sign):
        if sign == 0:
            return total
        if total is None:
            return term if sign > 0 else -term
        return total + term if sign > 0 else total - term

    for i in range(27):
        f = load(i)
        rho = acc(rho, f, 1)
        jx = acc(jx, f, VEL[i][0])
        jy = acc(jy, f, VEL[i][1])
        jz = acc(jz, f, VEL[i][2])
    return rho, jx, jy, jz


def velocity_kernel(pop_ref, row_in, rank_in, vel_ref, row_ref, rank_ref):
    row_ref[...] = row_in[...]
    rank_ref[...] = rank_in[...]
    comps = [[], [], []]
    for x in range(XD):
        rho, jx, jy, jz = moments(lambda i: pop_ref[i, x])
        for c, j in enumerate((jx, jy, jz)):
            comps[c].append(j / rho)
    low = jnp.concatenate([v for comp in comps for v in comp], axis=0)
    high = pltpu.roll(low, NY - 1, 1)
    hi, lo = split(jnp.concatenate([low, high], axis=0))
    vel_ref[...] = jnp.concatenate([hi, lo], axis=0)


def signed(vec, c):
    total = None
    for v, s in zip(vec, c):
        if s:
            term = v if s > 0 else -v
            total = term if total is None else total + term
    return total


def force_kernel(recv_ref, vel_ref, pop_ref, post_ref, back_hbm, pair_ref, cross_ref, back_ref, sem):
    first = (lax.axis_index("blk") & 1) == 0
    table = jnp.transpose(recv_ref[...])
    feat = [table[8 * k : 8 * k + 8] for k in range(8)]
    ox, oy, oz = feat[0], feat[1], feat[2]
    valid = feat[7]
    cell = feat[6].astype(jnp.int32)
    y_low = cell & (NY - 1)
    rest = cell >> 7
    x_low = jnp.where(rest >= 7, 1, 0) + jnp.where(rest >= 14, 1, 0)
    z_low = rest - 7 * x_low
    wx = [
        jnp.where(x_low == x, 1.0 - ox, 0.0) + jnp.where(x_low == x - 1, ox, 0.0)
        for x in range(XD)
    ]
    rows = iota((NY, NB), 0)
    zrow = iota((ZD, NB), 0)
    hot = [jnp.where(rows == y_low[r : r + 1], 1.0, 0.0).astype(BF16) for r in range(CAP)]
    hot = jnp.concatenate(hot, axis=1)
    looked = dot_nn(vel_ref[...], hot)
    looked = looked[:192] + looked[192:]
    pulls = [[], [], []]
    near, far = [], []
    for r in range(CAP):
        one = slice(r, r + 1)
        zl, fz, fy = z_low[one], oz[one], oy[one]
        wz = jnp.where(zrow == zl, 1.0 - fz, 0.0) + jnp.where(zrow == zl + 1, fz, 0.0)
        wz0, wz1 = wz * (1.0 - fy), wz * fy
        w0 = [wz0 * wx[x][one] for x in range(XD)]
        w1 = [wz1 * wx[x][one] for x in range(XD)]
        lanes = slice(NB * r, NB * r + NB)
        col0, col1 = [], []
        for c in range(3):
            total = None
            for x in range(XD):
                at = 32 * c + 8 * x
                term = looked[at : at + 8, lanes] * w0[x] + looked[96 + at : 104 + at, lanes] * w1[x]
                total = term if total is None else total + term
            interp = jnp.sum(total, axis=0, keepdims=True)
            pull = 2.0 * (feat[3 + c][one] - interp) * valid[one]
            pulls[c].append(pull)
            col0 += [w0[x] * pull for x in range(XD)]
            col1 += [w1[x] * pull for x in range(XD)]
        near.append(jnp.concatenate(col0, axis=0))
        far.append(jnp.concatenate(col1, axis=0))
    reply = jnp.concatenate([p for comp in pulls for p in comp] + [jnp.zeros((NB - 24, NB), F32)], axis=0)
    back_ref[...] = jnp.transpose(reply)
    sent = pltpu.make_async_copy(back_ref, back_hbm, sem)
    sent.start()
    amount = jnp.concatenate([jnp.concatenate(near, axis=1), jnp.concatenate(far, axis=1)], axis=0)
    hi, lo = split(amount)
    field = dot_nt(hi, hot) + dot_nt(lo, hot)
    field = field[:96] + pltpu.roll(field[96:], 1, 1)
    for x in range(XD):
        rho, jx, jy, jz = moments(lambda i: pop_ref[i, x])
        force = [field[32 * c + 8 * x : 32 * c + 8 * x + 8] for c in range(3)]
        inv = 1.0 / rho
        u = [(j + 0.5 * f) * inv for j, f in zip((jx, jy, jz), force)]
        usq = u[0] * u[0] + u[1] * u[1] + u[2] * u[2]
        uf = u[0] * force[0] + u[1] * force[1] + u[2] * force[2]
        base = 1.6 * rho * (1.0 - 1.5 * usq) - 0.6 * uf
        ru = [rho * v for v in u]
        g = [4.8 * a + 0.6 * f for a, f in zip(ru, force)]
        h = [7.2 * a + 1.8 * f for a, f in zip(ru, force)]
        for i in range(13, 27):
            if i == 13:
                posts = ((13, WTS[13] * base),)
            else:
                c = VEL[i]
                even = base + signed(u, c) * signed(h, c)
                odd = signed(g, c)
                posts = ((i, WTS[i] * (even + odd)), (26 - i, WTS[i] * (even - odd)))
            for k, term in posts:
                out = term - 0.6 * pop_ref[k, x]
                if VEL[k][1]:
                    out = pltpu.roll(out, VEL[k][1] % NY, 1)
                post_ref[k, x] = out


    for k in range(9):
        up, down = post_ref[UP_X[k], XD - 1], post_ref[DOWN_X[k], 0]
        pair_ref[k] = jnp.where(first, up, down)
        cross_ref[k] = jnp.where(first, down, up)
    sent.wait()


def shifted(even, post_ref, pair_ref, cross_ref, i, x):
    at = x - VEL[i][0]
    if at < 0:
        k = UP_X.index(i)
        return jnp.where(even, cross_ref[k], pair_ref[k])
    if at >= XD:
        k = DOWN_X.index(i)
        return jnp.where(even, pair_ref[k], cross_ref[k])
    return post_ref[i, at]


def edge_kernel(post_ref, high_ref, low_ref, pair_ref, cross_ref):
    even, even_z = (lax.axis_index("blk") & 1) == 0, (lax.axis_index("sub") & 1) == 0
    up, down = [], []
    for i in UP_Z:
        for x in range(XD):
            up.append(shifted(even, post_ref, low_ref, high_ref, i, x)[ZD - 1 :])
    for i in DOWN_Z:
        for x in range(XD):
            down.append(shifted(even, post_ref, low_ref, high_ref, i, x)[:1])
    up, down = jnp.concatenate(up, axis=0), jnp.concatenate(down, axis=0)
    pair_ref[...] = jnp.where(even_z, up, down)
    cross_ref[...] = jnp.where(even_z, down, up)


def last_kernel(post_ref, low_ref, high_ref, near_ref, far_ref, back_ref, row_ref, rank_ref, read_hbm, out_ref, read_ref, sems):
    even, even_z = (lax.axis_index("blk") & 1) == 0, (lax.axis_index("sub") & 1) == 0
    row = iota((ZD, NY), 0)
    near, far = near_ref[...], far_ref[...]
    below, above = jnp.where(even_z, far, near), jnp.where(even_z, near, far)
    copies = []
    for i in range(27):
        for x in range(XD):
            v = shifted(even, post_ref, low_ref, high_ref, i, x)
            if VEL[i][2] == 1:
                at = 4 * UP_Z.index(i) + x
                v = jnp.where(row == 0, below[at : at + 1], pltpu.roll(v, 1, 0))
            elif VEL[i][2] == -1:
                at = 4 * DOWN_Z.index(i) + x
                v = jnp.where(row == ZD - 1, above[at : at + 1], pltpu.roll(v, ZD - 1, 0))
            read_ref[i, x] = v
        if i % 9 == 8:
            part = pl.ds(i - 8, 9)
            copies.append(pltpu.make_async_copy(read_ref.at[part], read_hbm.at[part], sems.at[i // 9]))
            copies[-1].start()
    hot = jnp.where(iota((NB, M), 0) == row_ref[...], 1.0, 0.0).astype(BF16)
    hi, lo = split(jnp.transpose(back_ref[...])[:24])
    found = dot_nn(jnp.concatenate([hi, lo], axis=0), hot)
    found = found[:24] + found[24:]
    chosen = jnp.where(iota((CAP, M), 0) == rank_ref[...], 1.0, 0.0)
    for c in range(3):
        out_ref[c] = jnp.sum(found[8 * c : 8 * c + 8] * chosen, axis=0, keepdims=True)
    for copy in copies:
        copy.wait()


def call(kernel, outs, *args, cost=2_000_000, name=None, limit=LIMIT, far=(), scratch=()):
    return pl.pallas_call(
        kernel,
        out_shape=[jax.ShapeDtypeStruct(s, d) for s, d in outs],
        in_specs=[pl.BlockSpec(memory_space=pltpu.VMEM)] * len(args),
        out_specs=[pl.BlockSpec(memory_space=pltpu.HBM if k in far else pltpu.VMEM) for k in range(len(outs))],
        scratch_shapes=list(scratch),
        compiler_params=pltpu.CompilerParams(vmem_limit_bytes=limit),
        cost_estimate=pl.CostEstimate(flops=cost, bytes_accessed=cost, transcendentals=0),
        name=name,
    )(*args)


def exchange(x):
    order = [(k + TURN) % NB for k in range(NB)]
    out = lax.all_to_all(x.reshape(NB, 1, NY), "blk", split_axis=0, concat_axis=0, tiled=True, axis_index_groups=[order])
    return out.reshape(NB, NY)


def swaps(count, first):
    ends = [(k % count, (k + 1) % count) for k in range(first, count + first, 2)]
    return ends + [(b, a) for a, b in ends]


def body(populations, destination, base_cell, offsets, target):
    dest = destination.reshape(1, M)
    cell = base_cell.reshape(1, M)
    offs = offsets.reshape(3, 1, M)
    targ = target.reshape(3, 1, M)
    send, row, rank = call(pack_kernel, [((NB, NY), F32), ((1, M), jnp.int32), ((1, M), jnp.int32)], dest, cell, offs, targ, name="pack", limit=FIRST)
    recv = exchange(send)
    ints = ((1, M), jnp.int32)
    vel, row, rank = call(velocity_kernel, [((384, NY), BF16), ints, ints], populations, row, rank, name="velocity")
    face = (9, ZD, NY)
    post, back, pair, cross = call(
        force_kernel,
        [((27, XD, ZD, NY), F32), ((NB, NY), F32), (face, F32), (face, F32)],
        recv, vel, populations, name="force", far=(1,),
        scratch=[pltpu.VMEM((NB, NY), F32), pltpu.SemaphoreType.DMA],
    )
    reply = exchange(back)
    cross = lax.ppermute(cross, "blk", swaps(NB, 1))
    pair = lax.ppermute(pair, "blk", swaps(NB, 0))
    edge = (36, NY)
    near, far = call(edge_kernel, [(edge, F32), (edge, F32)], post, cross, pair, name="edge", cost=EDGE)
    near = lax.ppermute(near, "sub", swaps(4, 0))
    far = lax.ppermute(far, "sub", swaps(4, 1))
    whole = (27, XD, ZD, NY)
    read, pulled = call(
        last_kernel, [(whole, F32), ((3, 1, M), F32)],
        post, pair, cross, near, far, reply, row, rank, name="last", far=(0,),
        scratch=[pltpu.VMEM(whole, F32), pltpu.SemaphoreType.DMA((3,))],
    )
    return read, pulled.reshape(1, 1, 3, M)


def solution(mesh):
    in_specs = (
        P(None, "blk", "sub", None),
        P("blk", "sub", None, None),
        P("blk", "sub", None),
        P("blk", "sub", None, None),
        P("blk", "sub", None, None),
    )
    out_specs = (P(None, "blk", "sub", None), P("blk", "sub", None, None))
    return jax.shard_map(body, mesh=mesh, in_specs=in_specs, out_specs=out_specs, check_vma=False)
```

```python
import jax
import jax.numpy as jnp
import numpy as np
from jax import lax
from jax.experimental import pallas as pl
from jax.experimental.pallas import tpu as pltpu
from jax.sharding import PartitionSpec as P

CAP = 8
NB = 128
NY = 128
XD = 4
ZD = 8
M = 512
F32 = jnp.float32
BF16 = jnp.bfloat16
VEL = [(a, b, c) for a in (-1, 0, 1) for b in (-1, 0, 1) for c in (-1, 0, 1)]
WTS = [(8.0 / 27.0, 2.0 / 27.0, 1.0 / 54.0, 1.0 / 216.0)[abs(a) + abs(b) + abs(c)] for a, b, c in VEL]
UP_X = [i for i in range(27) if VEL[i][0] == 1]
DOWN_X = [i for i in range(27) if VEL[i][0] == -1]
UP_Z = [i for i in range(27) if VEL[i][2] == 1]
DOWN_Z = [i for i in range(27) if VEL[i][2] == -1]
LIMIT = 12 * 1024 * 1024
FIRST = 56 * 1024 * 1024
TURN = 127
BACK = 113
EDGE = 2_000_000_000


def iota(shape, dim):
    return lax.broadcasted_iota(jnp.int32, shape, dim)


def split(x):
    hi = x.astype(BF16)
    return hi, (x - hi.astype(F32)).astype(BF16)


def dot_nt(a, b):
    return lax.dot_general(a, b, (((1,), (1,)), ((), ())), preferred_element_type=F32)


def dot_nn(a, b):
    return lax.dot_general(a, b, (((1,), (0,)), ((), ())), preferred_element_type=F32)


def pack_kernel(dest_ref, cell_ref, offs_ref, targ_ref, send_ref, row_ref, rank_ref):
    owner = (dest_ref[...] - TURN) & (NB - 1)
    row_ref[...] = (dest_ref[...] - BACK) & (NB - 1)
    hot = jnp.where(iota((NB, M), 0) == owner, 1.0, 0.0)
    hot16 = hot.astype(BF16)
    blocks = [slice(NB * k, NB * k + NB) for k in range(M // NB)]
    column = iota((NB, 2 * NB), 1)
    before = jnp.where((iota((NB, 2 * NB), 0) < column) | (column >= NB), 1.0, 0.0).astype(BF16)
    count = dot_nn(jnp.concatenate([hot16[:, k] for k in blocks], axis=0), before)
    ranks, passed = [], 0.0
    for k in blocks:
        ranks.append(jnp.sum((count[k, :NB] + passed) * hot[:, k], axis=0, keepdims=True))
        passed = passed + count[k, NB:]
    rank = jnp.concatenate(ranks, axis=1).astype(jnp.int32)
    rank_ref[...] = rank
    chosen = jnp.where(iota((CAP, M), 0) == rank, 1.0, 0.0)
    feats = [offs_ref[k] for k in range(3)] + [targ_ref[k] for k in range(3)]
    feats += [cell_ref[...].astype(F32), jnp.ones((1, M), F32)]
    table = jnp.concatenate([chosen * f for f in feats], axis=0)
    hi, lo = split(table)
    packed = dot_nt(hot16, jnp.concatenate([hi, lo], axis=0))
    send_ref[...] = packed + pltpu.roll(packed, 64, 1)


def moments(load):
    rho = jx = jy = jz = None

    def acc(total, term, sign):
        if sign == 0:
            return total
        if total is None:
            return term if sign > 0 else -term
        return total + term if sign > 0 else total - term

    for i in range(27):
        f = load(i)
        rho = acc(rho, f, 1)
        jx = acc(jx, f, VEL[i][0])
        jy = acc(jy, f, VEL[i][1])
        jz = acc(jz, f, VEL[i][2])
    return rho, jx, jy, jz


def velocity_kernel(pop_ref, row_in, rank_in, vel_ref, row_ref, rank_ref):
    row_ref[...] = row_in[...]
    rank_ref[...] = rank_in[...]
    comps = [[], [], []]
    for x in range(XD):
        rho, jx, jy, jz = moments(lambda i: pop_ref[i, x])
        for c, j in enumerate((jx, jy, jz)):
            comps[c].append(j / rho)
    low = jnp.concatenate([v for comp in comps for v in comp], axis=0)
    high = pltpu.roll(low, NY - 1, 1)
    hi, lo = split(jnp.concatenate([low, high], axis=0))
    vel_ref[...] = jnp.concatenate([hi, lo], axis=0)


def signed(vec, c):
    total = None
    for v, s in zip(vec, c):
        if s:
            term = v if s > 0 else -v
            total = term if total is None else total + term
    return total


def force_kernel(recv_ref, vel_ref, pop_ref, post_ref, back_hbm, pair_ref, cross_ref, back_ref, sem):
    first = (lax.axis_index("blk") & 1) == 0
    table = jnp.transpose(recv_ref[...])
    feat = [table[8 * k : 8 * k + 8] for k in range(8)]
    ox, oy, oz = feat[0], feat[1], feat[2]
    valid = feat[7]
    cell = feat[6].astype(jnp.int32)
    y_low = cell & (NY - 1)
    rest = cell >> 7
    x_low = jnp.where(rest >= 7, 1, 0) + jnp.where(rest >= 14, 1, 0)
    z_low = rest - 7 * x_low
    wx = [
        jnp.where(x_low == x, 1.0 - ox, 0.0) + jnp.where(x_low == x - 1, ox, 0.0)
        for x in range(XD)
    ]
    rows = iota((NY, NB), 0)
    zrow = iota((ZD, NB), 0)
    hot = [jnp.where(rows == y_low[r : r + 1], 1.0, 0.0).astype(BF16) for r in range(CAP)]
    hot = jnp.concatenate(hot, axis=1)
    looked = dot_nn(vel_ref[...], hot)
    looked = looked[:192] + looked[192:]
    pulls = [[], [], []]
    near, far = [], []
    for r in range(CAP):
        one = slice(r, r + 1)
        zl, fz, fy = z_low[one], oz[one], oy[one]
        wz = jnp.where(zrow == zl, 1.0 - fz, 0.0) + jnp.where(zrow == zl + 1, fz, 0.0)
        wz0, wz1 = wz * (1.0 - fy), wz * fy
        w0 = [wz0 * wx[x][one] for x in range(XD)]
        w1 = [wz1 * wx[x][one] for x in range(XD)]
        lanes = slice(NB * r, NB * r + NB)
        col0, col1 = [], []
        for c in range(3):
            total = None
            for x in range(XD):
                at = 32 * c + 8 * x
                term = looked[at : at + 8, lanes] * w0[x] + looked[96 + at : 104 + at, lanes] * w1[x]
                total = term if total is None else total + term
            interp = jnp.sum(total, axis=0, keepdims=True)
            pull = 2.0 * (feat[3 + c][one] - interp) * valid[one]
            pulls[c].append(pull)
            col0 += [w0[x] * pull for x in range(XD)]
            col1 += [w1[x] * pull for x in range(XD)]
        near.append(jnp.concatenate(col0, axis=0))
        far.append(jnp.concatenate(col1, axis=0))
    reply = jnp.concatenate([p for comp in pulls for p in comp] + [jnp.zeros((NB - 24, NB), F32)], axis=0)
    if TURN != BACK:
        reply = pltpu.roll(reply, (TURN - BACK) % NB, 1)
    back_ref[...] = jnp.transpose(reply)
    sent = pltpu.make_async_copy(back_ref, back_hbm, sem)
    sent.start()
    amount = jnp.concatenate([jnp.concatenate(near, axis=1), jnp.concatenate(far, axis=1)], axis=0)
    hi, lo = split(amount)
    field = dot_nt(hi, hot) + dot_nt(lo, hot)
    field = field[:96] + pltpu.roll(field[96:], 1, 1)
    for x in range(XD):
        rho, jx, jy, jz = moments(lambda i: pop_ref[i, x])
        force = [field[32 * c + 8 * x : 32 * c + 8 * x + 8] for c in range(3)]
        inv = 1.0 / rho
        u = [(j + 0.5 * f) * inv for j, f in zip((jx, jy, jz), force)]
        usq = u[0] * u[0] + u[1] * u[1] + u[2] * u[2]
        uf = u[0] * force[0] + u[1] * force[1] + u[2] * force[2]
        base = 1.6 * rho * (1.0 - 1.5 * usq) - 0.6 * uf
        ru = [rho * v for v in u]
        g = [4.8 * a + 0.6 * f for a, f in zip(ru, force)]
        h = [7.2 * a + 1.8 * f for a, f in zip(ru, force)]
        for i in range(13, 27):
            if i == 13:
                posts = ((13, WTS[13] * base),)
            else:
                c = VEL[i]
                even = base + signed(u, c) * signed(h, c)
                odd = signed(g, c)
                posts = ((i, WTS[i] * (even + odd)), (26 - i, WTS[i] * (even - odd)))
            for k, term in posts:
                out = term - 0.6 * pop_ref[k, x]
                if VEL[k][1]:
                    out = pltpu.roll(out, VEL[k][1] % NY, 1)
                post_ref[k, x] = out


    for k in range(9):
        up, down = post_ref[UP_X[k], XD - 1], post_ref[DOWN_X[k], 0]
        pair_ref[k] = jnp.where(first, up, down)
        cross_ref[k] = jnp.where(first, down, up)
    sent.wait()


def shifted(even, post_ref, pair_ref, cross_ref, i, x):
    at = x - VEL[i][0]
    if at < 0:
        k = UP_X.index(i)
        return jnp.where(even, cross_ref[k], pair_ref[k])
    if at >= XD:
        k = DOWN_X.index(i)
        return jnp.where(even, pair_ref[k], cross_ref[k])
    return post_ref[i, at]


def edge_kernel(post_ref, high_ref, low_ref, pair_ref, cross_ref):
    even, even_z = (lax.axis_index("blk") & 1) == 0, (lax.axis_index("sub") & 1) == 0
    up, down = [], []
    for i in UP_Z:
        for x in range(XD):
            up.append(shifted(even, post_ref, low_ref, high_ref, i, x)[ZD - 1 :])
    for i in DOWN_Z:
        for x in range(XD):
            down.append(shifted(even, post_ref, low_ref, high_ref, i, x)[:1])
    up, down = jnp.concatenate(up, axis=0), jnp.concatenate(down, axis=0)
    pair_ref[...] = jnp.where(even_z, up, down)
    cross_ref[...] = jnp.where(even_z, down, up)


def last_kernel(post_ref, low_ref, high_ref, near_ref, far_ref, back_ref, row_ref, rank_ref, read_hbm, out_ref, read_ref, sems):
    even, even_z = (lax.axis_index("blk") & 1) == 0, (lax.axis_index("sub") & 1) == 0
    row = iota((ZD, NY), 0)
    near, far = near_ref[...], far_ref[...]
    below, above = jnp.where(even_z, far, near), jnp.where(even_z, near, far)
    copies = []
    for i in range(27):
        for x in range(XD):
            v = shifted(even, post_ref, low_ref, high_ref, i, x)
            if VEL[i][2] == 1:
                at = 4 * UP_Z.index(i) + x
                v = jnp.where(row == 0, below[at : at + 1], pltpu.roll(v, 1, 0))
            elif VEL[i][2] == -1:
                at = 4 * DOWN_Z.index(i) + x
                v = jnp.where(row == ZD - 1, above[at : at + 1], pltpu.roll(v, ZD - 1, 0))
            read_ref[i, x] = v
        if i % 9 == 8:
            part = pl.ds(i - 8, 9)
            copies.append(pltpu.make_async_copy(read_ref.at[part], read_hbm.at[part], sems.at[i // 9]))
            copies[-1].start()
    hot = jnp.where(iota((NB, M), 0) == row_ref[...], 1.0, 0.0).astype(BF16)
    hi, lo = split(jnp.transpose(back_ref[...])[:24])
    found = dot_nn(jnp.concatenate([hi, lo], axis=0), hot)
    found = found[:24] + found[24:]
    chosen = jnp.where(iota((CAP, M), 0) == rank_ref[...], 1.0, 0.0)
    for c in range(3):
        out_ref[c] = jnp.sum(found[8 * c : 8 * c + 8] * chosen, axis=0, keepdims=True)
    for copy in copies:
        copy.wait()


def call(kernel, outs, *args, cost=2_000_000, name=None, limit=LIMIT, far=(), scratch=()):
    return pl.pallas_call(
        kernel,
        out_shape=[jax.ShapeDtypeStruct(s, d) for s, d in outs],
        in_specs=[pl.BlockSpec(memory_space=pltpu.VMEM)] * len(args),
        out_specs=[pl.BlockSpec(memory_space=pltpu.HBM if k in far else pltpu.VMEM) for k in range(len(outs))],
        scratch_shapes=list(scratch),
        compiler_params=pltpu.CompilerParams(vmem_limit_bytes=limit),
        cost_estimate=pl.CostEstimate(flops=cost, bytes_accessed=cost, transcendentals=0),
        name=name,
    )(*args)


def exchange(x, turn):
    order = [(k + turn) % NB for k in range(NB)]
    out = lax.all_to_all(x.reshape(NB, 1, NY), "blk", split_axis=0, concat_axis=0, tiled=True, axis_index_groups=[order])
    return out.reshape(NB, NY)


def swaps(count, first):
    ends = [(k % count, (k + 1) % count) for k in range(first, count + first, 2)]
    return ends + [(b, a) for a, b in ends]


def body(populations, destination, base_cell, offsets, target):
    dest = destination.reshape(1, M)
    cell = base_cell.reshape(1, M)
    offs = offsets.reshape(3, 1, M)
    targ = target.reshape(3, 1, M)
    send, row, rank = call(pack_kernel, [((NB, NY), F32), ((1, M), jnp.int32), ((1, M), jnp.int32)], dest, cell, offs, targ, name="pack", limit=FIRST)
    recv = exchange(send, TURN)
    ints = ((1, M), jnp.int32)
    vel, row, rank = call(velocity_kernel, [((384, NY), BF16), ints, ints], populations, row, rank, name="velocity")
    face = (9, ZD, NY)
    post, back, pair, cross = call(
        force_kernel,
        [((27, XD, ZD, NY), F32), ((NB, NY), F32), (face, F32), (face, F32)],
        recv, vel, populations, name="force", far=(1,),
        scratch=[pltpu.VMEM((NB, NY), F32), pltpu.SemaphoreType.DMA],
    )
    reply = exchange(back, BACK)
    cross = lax.ppermute(cross, "blk", swaps(NB, 1))
    pair = lax.ppermute(pair, "blk", swaps(NB, 0))
    edge = (36, NY)
    near, far = call(edge_kernel, [(edge, F32), (edge, F32)], post, cross, pair, name="edge", cost=EDGE)
    near = lax.ppermute(near, "sub", swaps(4, 0))
    far = lax.ppermute(far, "sub", swaps(4, 1))
    whole = (27, XD, ZD, NY)
    read, pulled = call(
        last_kernel, [(whole, F32), ((3, 1, M), F32)],
        post, pair, cross, near, far, reply, row, rank, name="last", far=(0,),
        scratch=[pltpu.VMEM(whole, F32), pltpu.SemaphoreType.DMA((3,))],
    )
    return read, pulled.reshape(1, 1, 3, M)


def solution(mesh):
    in_specs = (
        P(None, "blk", "sub", None),
        P("blk", "sub", None, None),
        P("blk", "sub", None),
        P("blk", "sub", None, None),
        P("blk", "sub", None, None),
    )
    out_specs = (P(None, "blk", "sub", None), P("blk", "sub", None, None))
    return jax.shard_map(body, mesh=mesh, in_specs=in_specs, out_specs=out_specs, check_vma=False)
```

```python
import jax
import jax.numpy as jnp
import numpy as np
from jax import lax
from jax.experimental import pallas as pl
from jax.experimental.pallas import tpu as pltpu
from jax.sharding import PartitionSpec as P

CAP = 8
NB = 128
NY = 128
XD = 4
ZD = 8
M = 512
F32 = jnp.float32
BF16 = jnp.bfloat16
VEL = [(a, b, c) for a in (-1, 0, 1) for b in (-1, 0, 1) for c in (-1, 0, 1)]
WTS = [(8.0 / 27.0, 2.0 / 27.0, 1.0 / 54.0, 1.0 / 216.0)[abs(a) + abs(b) + abs(c)] for a, b, c in VEL]
UP_X = [i for i in range(27) if VEL[i][0] == 1]
DOWN_X = [i for i in range(27) if VEL[i][0] == -1]
UP_Z = [i for i in range(27) if VEL[i][2] == 1]
DOWN_Z = [i for i in range(27) if VEL[i][2] == -1]
LIMIT = 12 * 1024 * 1024
FIRST = 56 * 1024 * 1024
TURN = 127
BACK = 113
EDGE = 2_000_000_000


def iota(shape, dim):
    return lax.broadcasted_iota(jnp.int32, shape, dim)


def split(x):
    hi = x.astype(BF16)
    return hi, (x - hi.astype(F32)).astype(BF16)


def dot_nt(a, b):
    return lax.dot_general(a, b, (((1,), (1,)), ((), ())), preferred_element_type=F32)


def dot_nn(a, b):
    return lax.dot_general(a, b, (((1,), (0,)), ((), ())), preferred_element_type=F32)


def pack_kernel(dest_ref, cell_ref, offs_ref, targ_ref, send_ref, row_ref, rank_ref):
    owner = (dest_ref[...] - TURN) & (NB - 1)
    row_ref[...] = (dest_ref[...] - BACK) & (NB - 1)
    hot = jnp.where(iota((NB, M), 0) == owner, 1.0, 0.0)
    hot16 = hot.astype(BF16)
    blocks = [slice(NB * k, NB * k + NB) for k in range(M // NB)]
    column = iota((NB, 2 * NB), 1)
    before = jnp.where((iota((NB, 2 * NB), 0) < column) | (column >= NB), 1.0, 0.0).astype(BF16)
    count = dot_nn(jnp.concatenate([hot16[:, k] for k in blocks], axis=0), before)
    ranks, passed = [], 0.0
    for k in blocks:
        ranks.append(jnp.sum((count[k, :NB] + passed) * hot[:, k], axis=0, keepdims=True))
        passed = passed + count[k, NB:]
    rank = jnp.concatenate(ranks, axis=1).astype(jnp.int32)
    rank_ref[...] = rank
    chosen = jnp.where(iota((CAP, M), 0) == rank, 1.0, 0.0)
    feats = [offs_ref[k] for k in range(3)] + [targ_ref[k] for k in range(3)]
    feats += [cell_ref[...].astype(F32), jnp.ones((1, M), F32)]
    table = jnp.concatenate([chosen * f for f in feats], axis=0)
    hi, lo = split(table)
    packed = dot_nt(hot16, jnp.concatenate([hi, lo], axis=0))
    send_ref[...] = packed + pltpu.roll(packed, 64, 1)


def moments(load):
    rho = jx = jy = jz = None

    def acc(total, term, sign):
        if sign == 0:
            return total
        if total is None:
            return term if sign > 0 else -term
        return total + term if sign > 0 else total - term

    for i in range(27):
        f = load(i)
        rho = acc(rho, f, 1)
        jx = acc(jx, f, VEL[i][0])
        jy = acc(jy, f, VEL[i][1])
        jz = acc(jz, f, VEL[i][2])
    return rho, jx, jy, jz


def velocity_kernel(pop_ref, row_in, rank_in, vel_ref, row_ref, rank_ref, mom_ref):
    row_ref[...] = row_in[...]
    rank_ref[...] = rank_in[...]
    comps = [[], [], []]
    for x in range(XD):
        rho, jx, jy, jz = moments(lambda i: pop_ref[i, x])
        for k, v in enumerate((rho, jx, jy, jz, 1.0 / rho)):
            mom_ref[k, x] = v
        for c, j in enumerate((jx, jy, jz)):
            comps[c].append(j / rho)
    low = jnp.concatenate([v for comp in comps for v in comp], axis=0)
    high = pltpu.roll(low, NY - 1, 1)
    hi, lo = split(jnp.concatenate([low, high], axis=0))
    vel_ref[...] = jnp.concatenate([hi, lo], axis=0)


def signed(vec, c):
    total = None
    for v, s in zip(vec, c):
        if s:
            term = v if s > 0 else -v
            total = term if total is None else total + term
    return total


def force_kernel(recv_ref, vel_ref, pop_ref, mom_ref, post_ref, back_hbm, pair_ref, cross_ref, back_ref, sem):
    first = (lax.axis_index("blk") & 1) == 0
    table = jnp.transpose(recv_ref[...])
    feat = [table[8 * k : 8 * k + 8] for k in range(8)]
    ox, oy, oz = feat[0], feat[1], feat[2]
    valid = feat[7]
    cell = feat[6].astype(jnp.int32)
    y_low = cell & (NY - 1)
    rest = cell >> 7
    x_low = jnp.where(rest >= 7, 1, 0) + jnp.where(rest >= 14, 1, 0)
    z_low = rest - 7 * x_low
    wx = [
        jnp.where(x_low == x, 1.0 - ox, 0.0) + jnp.where(x_low == x - 1, ox, 0.0)
        for x in range(XD)
    ]
    rows = iota((NY, NB), 0)
    zrow = iota((ZD, NB), 0)
    hot = [jnp.where(rows == y_low[r : r + 1], 1.0, 0.0).astype(BF16) for r in range(CAP)]
    hot = jnp.concatenate(hot, axis=1)
    looked = dot_nn(vel_ref[...], hot)
    looked = looked[:192] + looked[192:]
    pulls = [[], [], []]
    near, far = [], []
    for r in range(CAP):
        one = slice(r, r + 1)
        zl, fz, fy = z_low[one], oz[one], oy[one]
        wz = jnp.where(zrow == zl, 1.0 - fz, 0.0) + jnp.where(zrow == zl + 1, fz, 0.0)
        wz0, wz1 = wz * (1.0 - fy), wz * fy
        w0 = [wz0 * wx[x][one] for x in range(XD)]
        w1 = [wz1 * wx[x][one] for x in range(XD)]
        lanes = slice(NB * r, NB * r + NB)
        col0, col1 = [], []
        for c in range(3):
            total = None
            for x in range(XD):
                at = 32 * c + 8 * x
                term = looked[at : at + 8, lanes] * w0[x] + looked[96 + at : 104 + at, lanes] * w1[x]
                total = term if total is None else total + term
            interp = jnp.sum(total, axis=0, keepdims=True)
            pull = 2.0 * (feat[3 + c][one] - interp) * valid[one]
            pulls[c].append(pull)
            col0 += [w0[x] * pull for x in range(XD)]
            col1 += [w1[x] * pull for x in range(XD)]
        near.append(jnp.concatenate(col0, axis=0))
        far.append(jnp.concatenate(col1, axis=0))
    reply = jnp.concatenate([p for comp in pulls for p in comp] + [jnp.zeros((NB - 24, NB), F32)], axis=0)
    if TURN != BACK:
        reply = pltpu.roll(reply, (TURN - BACK) % NB, 1)
    back_ref[...] = jnp.transpose(reply)
    sent = pltpu.make_async_copy(back_ref, back_hbm, sem)
    sent.start()
    amount = jnp.concatenate([jnp.concatenate(near, axis=1), jnp.concatenate(far, axis=1)], axis=0)
    hi, lo = split(amount)
    field = dot_nt(hi, hot) + dot_nt(lo, hot)
    field = field[:96] + pltpu.roll(field[96:], 1, 1)
    for x in range(XD):
        rho, jx, jy, jz, inv = [mom_ref[k, x] for k in range(5)]
        force = [field[32 * c + 8 * x : 32 * c + 8 * x + 8] for c in range(3)]
        u = [(j + 0.5 * f) * inv for j, f in zip((jx, jy, jz), force)]
        usq = u[0] * u[0] + u[1] * u[1] + u[2] * u[2]
        uf = u[0] * force[0] + u[1] * force[1] + u[2] * force[2]
        base = 1.6 * rho * (1.0 - 1.5 * usq) - 0.6 * uf
        ru = [rho * v for v in u]
        g = [4.8 * a + 0.6 * f for a, f in zip(ru, force)]
        h = [7.2 * a + 1.8 * f for a, f in zip(ru, force)]
        for i in range(13, 27):
            if i == 13:
                posts = ((13, WTS[13] * base),)
            else:
                c = VEL[i]
                even = base + signed(u, c) * signed(h, c)
                odd = signed(g, c)
                posts = ((i, WTS[i] * (even + odd)), (26 - i, WTS[i] * (even - odd)))
            for k, term in posts:
                out = term - 0.6 * pop_ref[k, x]
                if VEL[k][1]:
                    out = pltpu.roll(out, VEL[k][1] % NY, 1)
                post_ref[k, x] = out


    for k in range(9):
        up, down = post_ref[UP_X[k], XD - 1], post_ref[DOWN_X[k], 0]
        pair_ref[k] = jnp.where(first, up, down)
        cross_ref[k] = jnp.where(first, down, up)
    sent.wait()


def shifted(even, post_ref, pair_ref, cross_ref, i, x):
    at = x - VEL[i][0]
    if at < 0:
        k = UP_X.index(i)
        return jnp.where(even, cross_ref[k], pair_ref[k])
    if at >= XD:
        k = DOWN_X.index(i)
        return jnp.where(even, pair_ref[k], cross_ref[k])
    return post_ref[i, at]


def edge_kernel(post_ref, high_ref, low_ref, pair_ref, cross_ref):
    even, even_z = (lax.axis_index("blk") & 1) == 0, (lax.axis_index("sub") & 1) == 0
    up, down = [], []
    for i in UP_Z:
        for x in range(XD):
            up.append(shifted(even, post_ref, low_ref, high_ref, i, x)[ZD - 1 :])
    for i in DOWN_Z:
        for x in range(XD):
            down.append(shifted(even, post_ref, low_ref, high_ref, i, x)[:1])
    up, down = jnp.concatenate(up, axis=0), jnp.concatenate(down, axis=0)
    pair_ref[...] = jnp.where(even_z, up, down)
    cross_ref[...] = jnp.where(even_z, down, up)


def last_kernel(post_ref, low_ref, high_ref, near_ref, far_ref, back_ref, row_ref, rank_ref, read_hbm, out_ref, read_ref, sems):
    even, even_z = (lax.axis_index("blk") & 1) == 0, (lax.axis_index("sub") & 1) == 0
    row = iota((ZD, NY), 0)
    near, far = near_ref[...], far_ref[...]
    below, above = jnp.where(even_z, far, near), jnp.where(even_z, near, far)
    copies = []
    for i in range(27):
        for x in range(XD):
            v = shifted(even, post_ref, low_ref, high_ref, i, x)
            if VEL[i][2] == 1:
                at = 4 * UP_Z.index(i) + x
                v = jnp.where(row == 0, below[at : at + 1], pltpu.roll(v, 1, 0))
            elif VEL[i][2] == -1:
                at = 4 * DOWN_Z.index(i) + x
                v = jnp.where(row == ZD - 1, above[at : at + 1], pltpu.roll(v, ZD - 1, 0))
            read_ref[i, x] = v
        if i % 9 == 8:
            part = pl.ds(i - 8, 9)
            copies.append(pltpu.make_async_copy(read_ref.at[part], read_hbm.at[part], sems.at[i // 9]))
            copies[-1].start()
    hot = jnp.where(iota((NB, M), 0) == row_ref[...], 1.0, 0.0).astype(BF16)
    hi, lo = split(jnp.transpose(back_ref[...])[:24])
    found = dot_nn(jnp.concatenate([hi, lo], axis=0), hot)
    found = found[:24] + found[24:]
    chosen = jnp.where(iota((CAP, M), 0) == rank_ref[...], 1.0, 0.0)
    for c in range(3):
        out_ref[c] = jnp.sum(found[8 * c : 8 * c + 8] * chosen, axis=0, keepdims=True)
    for copy in copies:
        copy.wait()


def call(kernel, outs, *args, cost=2_000_000, name=None, limit=LIMIT, far=(), scratch=()):
    return pl.pallas_call(
        kernel,
        out_shape=[jax.ShapeDtypeStruct(s, d) for s, d in outs],
        in_specs=[pl.BlockSpec(memory_space=pltpu.VMEM)] * len(args),
        out_specs=[pl.BlockSpec(memory_space=pltpu.HBM if k in far else pltpu.VMEM) for k in range(len(outs))],
        scratch_shapes=list(scratch),
        compiler_params=pltpu.CompilerParams(vmem_limit_bytes=limit),
        cost_estimate=pl.CostEstimate(flops=cost, bytes_accessed=cost, transcendentals=0),
        name=name,
    )(*args)


def exchange(x, turn):
    order = [(k + turn) % NB for k in range(NB)]
    out = lax.all_to_all(x.reshape(NB, 1, NY), "blk", split_axis=0, concat_axis=0, tiled=True, axis_index_groups=[order])
    return out.reshape(NB, NY)


def swaps(count, first):
    ends = [(k % count, (k + 1) % count) for k in range(first, count + first, 2)]
    return ends + [(b, a) for a, b in ends]


def body(populations, destination, base_cell, offsets, target):
    dest = destination.reshape(1, M)
    cell = base_cell.reshape(1, M)
    offs = offsets.reshape(3, 1, M)
    targ = target.reshape(3, 1, M)
    send, row, rank = call(pack_kernel, [((NB, NY), F32), ((1, M), jnp.int32), ((1, M), jnp.int32)], dest, cell, offs, targ, name="pack", limit=FIRST)
    recv = exchange(send, TURN)
    ints = ((1, M), jnp.int32)
    vel, row, rank, mom = call(velocity_kernel, [((384, NY), BF16), ints, ints, ((5, XD, ZD, NY), F32)], populations, row, rank, name="velocity")
    face = (9, ZD, NY)
    post, back, pair, cross = call(
        force_kernel,
        [((27, XD, ZD, NY), F32), ((NB, NY), F32), (face, F32), (face, F32)],
        recv, vel, populations, mom, name="force", far=(1,),
        scratch=[pltpu.VMEM((NB, NY), F32), pltpu.SemaphoreType.DMA],
    )
    reply = exchange(back, BACK)
    cross = lax.ppermute(cross, "blk", swaps(NB, 1))
    pair = lax.ppermute(pair, "blk", swaps(NB, 0))
    edge = (36, NY)
    near, far = call(edge_kernel, [(edge, F32), (edge, F32)], post, cross, pair, name="edge", cost=EDGE)
    near = lax.ppermute(near, "sub", swaps(4, 0))
    far = lax.ppermute(far, "sub", swaps(4, 1))
    whole = (27, XD, ZD, NY)
    read, pulled = call(
        last_kernel, [(whole, F32), ((3, 1, M), F32)],
        post, pair, cross, near, far, reply, row, rank, name="last", far=(0,),
        scratch=[pltpu.VMEM(whole, F32), pltpu.SemaphoreType.DMA((3,))],
    )
    return read, pulled.reshape(1, 1, 3, M)


def solution(mesh):
    in_specs = (
        P(None, "blk", "sub", None),
        P("blk", "sub", None, None),
        P("blk", "sub", None),
        P("blk", "sub", None, None),
        P("blk", "sub", None, None),
    )
    out_specs = (P(None, "blk", "sub", None), P("blk", "sub", None, None))
    return jax.shard_map(body, mesh=mesh, in_specs=in_specs, out_specs=out_specs, check_vma=False)
```
